512 devices in a mesh: pipe: 32 (over y_lo, z), dp: 8 (over x, y_hi), mp: 2 (over core).
Axes of the slice: x: 4, y: 8 (y_hi: 2, y_lo: 4; y = y_hi * 4 + y_lo), z: 8, core: 2. Of those that a mesh axis runs over, the one named last changes fastest.
Arguments:
- activations: bfloat16 [8, 128, 7168], P('dp', 'pipe', 'mp'), may hold values from -6 to 6
- cotangent: bfloat16 [8, 128, 7168], P('dp', 'pipe', 'mp'), may hold values from -6 to 6
- squeeze_old: bfloat16 [32, 7168, 64], P('pipe', 'mp'), may hold values from -5 to 5
- expand_old: bfloat16 [32, 64, 7168], P('pipe', None, 'mp'), may hold values from -5 to 5
- squeeze_late: bfloat16 [8, 32, 7168, 64], P('dp', 'pipe', 'mp'), may hold values from -6 to 6
- expand_late: bfloat16 [8, 32, 64, 7168], P('dp', 'pipe', None, 'mp'), may hold values from -6 to 6
- stash_inputs: bfloat16 [8, 32, 8, 16, 7168], P('dp', 'pipe', None, None, 'mp'), may hold values from -6 to 6
- forward_in: bfloat16 [8, 32, 16, 7168], P('dp', 'pipe', None, 'mp'), may hold values from -6 to 6
- backward_in: bfloat16 [8, 32, 16, 7168], P('dp', 'pipe', None, 'mp'), may hold values from -6 to 6
Outputs:
- squeeze_new: bfloat16 [32, 7168, 64], P('pipe', 'mp')
- expand_new: bfloat16 [32, 64, 7168], P('pipe', None, 'mp')
- squeeze_grad: bfloat16 [8, 32, 7168, 64], P('dp', 'pipe', 'mp')
- expand_grad: bfloat16 [8, 32, 64, 7168], P('dp', 'pipe', None, 'mp')
- forward_carry: bfloat16 [8, 32, 16, 7168], P('dp', 'pipe', None, 'mp')
- backward_carry: bfloat16 [8, 32, 16, 7168], P('dp', 'pipe', None, 'mp')
The draws below stay inside these ranges and needn't reach their ends.
All inputs are finite; a program needn't handle non-finite values.
Results may differ from the reference program's by a relative error of at most 0.009.
Values may be sent and summed in bfloat16 or wider, within the bound.
A program may use at most 64 MiB of HBM per device.

```python
import math
import jax
import jax.numpy as jnp
from jax import lax

D = 7168
RANK = 64
ROWS = 16
TICKS = 8
TOK_REP = 128
LAYERS = 32
N_DP = 8


def levels(rng, shape, pieces, smallest, top_value):
    gain = 1.0
    for dim, parts in pieces:
        draws = jax.random.uniform(jax.random.fold_in(jax.random.fold_in(rng, 6), dim), (parts,), jnp.float32, smallest / len(pieces), top_value / len(pieces))
        gain = gain * jnp.repeat(jnp.exp(draws), shape[dim] // parts).reshape((-1,) + (1,) * (len(shape) - 1 - dim))
    return gain


def noise(key, extent, spread, limit, split=(), kind=jnp.bfloat16):
    gain = levels(key, extent, split, -0.22, 0.18) if split else 1.0
    array = jax.random.normal(key, extent, jnp.float32) * spread * gain
    return jnp.minimum(jnp.maximum(array, -limit), limit).astype(kind)


def setup_inputs(seed: int = 0) -> dict:
    key_of = jax.random.split(jax.random.key(seed), 10)
    activations = noise(key_of[0], (N_DP, TOK_REP, D), 1.0, 6.0, ((0, 8), (1, 32), (2, 2)))
    cotangent = noise(key_of[1], (N_DP, TOK_REP, D), 1.0, 6.0, ((0, 8), (1, 32), (2, 2)))
    squeeze_old = noise(key_of[2], (LAYERS, D, RANK), 1.0, 5.0, ((0, 32), (1, 2)))
    expand_old = noise(key_of[3], (LAYERS, RANK, D), 1.0, 5.0, ((0, 32), (2, 2)))
    squeeze_late = noise(key_of[4], (N_DP, LAYERS, D, RANK), 1.0, 6.0, ((0, 8), (1, 32), (2, 2)))
    expand_late = noise(key_of[5], (N_DP, LAYERS, RANK, D), 1.0, 6.0, ((0, 8), (1, 32), (3, 2)))
    stash_inputs = noise(key_of[6], (N_DP, LAYERS, TICKS, ROWS, D), 1.0, 6.0, ((0, 8), (1, 32), (4, 2)))
    forward_in = noise(key_of[7], (N_DP, LAYERS, ROWS, D), 1.0, 6.0, ((0, 8), (1, 32), (3, 2)))
    backward_in = noise(key_of[8], (N_DP, LAYERS, ROWS, D), 1.0, 6.0, ((0, 8), (1, 32), (3, 2)))
    return {"activations": activations, "cotangent": cotangent, "squeeze_old": squeeze_old, "expand_old": expand_old, "squeeze_late": squeeze_late, "expand_late": expand_late, "stash_inputs": stash_inputs, "forward_in": forward_in, "backward_in": backward_in}


BRANCH_SCALE = 0.25
STEP_RATE = 0.5

def activate(values):
    return jax.nn.gelu(values, approximate=True)

def section_forward(inputs, squeeze_old, expand_old):
    inv_width = 1.0 / math.sqrt(D)
    inv_rank = BRANCH_SCALE / math.sqrt(RANK)
    hidden = jnp.einsum('srd,sdk->srk', inputs.astype(jnp.float32), squeeze_old.astype(jnp.float32)) * inv_width
    gated = activate(hidden).astype(jnp.bfloat16)
    branch = jnp.einsum('srk,skd->srd', gated.astype(jnp.float32), expand_old.astype(jnp.float32)) * inv_rank
    return (inputs.astype(jnp.float32) + branch).astype(jnp.bfloat16)

def section_backward(saved, upstream, squeeze_old, expand_old):
    inv_width = 1.0 / math.sqrt(D)
    inv_rank = BRANCH_SCALE / math.sqrt(RANK)
    again = jnp.einsum('srd,sdk->srk', saved.astype(jnp.float32), squeeze_old.astype(jnp.float32)) * inv_width
    gate_grad = jnp.einsum('srd,skd->srk', upstream.astype(jnp.float32), expand_old.astype(jnp.float32)) * inv_rank
    regated, pullback = jax.vjp(activate, again)
    hidden_grad = pullback(gate_grad)[0].astype(jnp.bfloat16)
    regated = regated.astype(jnp.bfloat16)
    expand_term = jnp.einsum('srk,srd->skd', regated.astype(jnp.float32), upstream.astype(jnp.float32)) * inv_rank
    squeeze_term = jnp.einsum('srd,srk->sdk', saved.astype(jnp.float32), hidden_grad.astype(jnp.float32)) * inv_width
    back = jnp.einsum('srk,sdk->srd', hidden_grad.astype(jnp.float32), squeeze_old.astype(jnp.float32)) * inv_width
    downstream = (upstream.astype(jnp.float32) + back).astype(jnp.bfloat16)
    return (downstream, squeeze_term, expand_term)

def replica_pass(feeds, targets, stash, first_fwd, first_bwd, squeeze_old, expand_old):
    section_ids = jnp.arange(LAYERS, dtype=jnp.int32)
    lags = (2 * LAYERS - 1 - 2 * section_ids).astype(jnp.int32)
    squeeze_sum = jnp.zeros((LAYERS, D, RANK), jnp.float32)
    expand_sum = jnp.zeros((LAYERS, RANK, D), jnp.float32)
    history = []
    outputs = None
    downstream = None
    for tick in range(TICKS):
        fed = feeds[tick * ROWS:(tick + 1) * ROWS][None]
        target = targets[tick * ROWS:(tick + 1) * ROWS][None]
        if tick == 0:
            layer_in = jnp.concatenate([fed, first_fwd[1:]], axis=0)
            upstream = jnp.concatenate([first_bwd[:-1], target], axis=0)
        else:
            layer_in = jnp.concatenate([fed, outputs[:-1]], axis=0)
            upstream = jnp.concatenate([downstream[1:], target], axis=0)
        history.append(layer_in)
        outputs = section_forward(layer_in, squeeze_old, expand_old)
        stacked = jnp.stack(history)
        back = (tick - lags).astype(jnp.int32)
        picked = stacked[jnp.clip(back, 0, tick).astype(jnp.int32), section_ids]
        saved = jnp.where((back >= 0)[:, None, None], picked, stash[:, tick])
        downstream, squeeze_term, expand_term = section_backward(saved, upstream, squeeze_old, expand_old)
        squeeze_sum = squeeze_sum + squeeze_term
        expand_sum = expand_sum + expand_term
    return (squeeze_sum.astype(jnp.bfloat16), expand_sum.astype(jnp.bfloat16), outputs, downstream)

def reference(activations, cotangent, squeeze_old, expand_old, squeeze_late, expand_late, stash_inputs, forward_in, backward_in):
    squeeze_new = (squeeze_old.astype(jnp.float32) - STEP_RATE * lax.optimization_barrier(jnp.sum(squeeze_late.astype(jnp.float32), axis=0)) / N_DP).astype(jnp.bfloat16)
    expand_new = (expand_old.astype(jnp.float32) - STEP_RATE * lax.optimization_barrier(jnp.sum(expand_late.astype(jnp.float32), axis=0)) / N_DP).astype(jnp.bfloat16)

    def one_replica(group):
        return replica_pass(group[0], group[1], group[2], group[3], group[4], squeeze_old, expand_old)
    squeeze_grad, expand_grad, forward_carry, backward_carry = lax.map(one_replica, (activations, cotangent, stash_inputs, forward_in, backward_in))
    return (squeeze_new, expand_new, squeeze_grad, expand_grad, forward_carry, backward_carry)
```

```python
import functools
import math

import jax
import jax.numpy as jnp
from jax import lax
from jax.experimental import pallas as pl
from jax.experimental.pallas import tpu as pltpu
from jax.sharding import PartitionSpec as P

D = 7168
RANK = 64
TICKS = 8
ROWS = 16
BRANCH_SCALE = 0.25
STEP_RATE = 0.5
CHUNKS = 2

F32 = jnp.float32
BF16 = jnp.bfloat16
MESH = pl.DeviceIdType.MESH
GELU_A = math.sqrt(2.0 / math.pi)
GELU_B = 0.044715


def gelu(v):
    return 0.5 * v * (1.0 + jnp.tanh(GELU_A * (v + GELU_B * (v * v * v))))


def gelu_slope(v):
    t = jnp.tanh(GELU_A * (v + GELU_B * (v * v * v)))
    inner = GELU_A * (1.0 + 3.0 * GELU_B * (v * v))
    return 0.5 * (1.0 + t) + 0.5 * v * ((1.0 - t * t) * inner)


def rows_by_rows(left, right):
    return lax.dot_general(left, right, (((1,), (1,)), ((), ())), preferred_element_type=F32)


def times(left, right):
    return jnp.dot(left, right, preferred_element_type=F32)


def window(
    sections, replicas, half,
    act, cot, sq, ex, lsq, lex, stash, fin, bin_,
    nsq, nex, gsq, gex, fco, bco,
    ss, ee, st, first, a_in, g_in, a_out, g_out, a_peer, g_peer, carry_peer,
    feed, feed_rows, again, again_peer, hg, rg, hg_peer, rg_peer, late, r1, p1, r2, p2, ry, new,
    grads, carry,
    load_sem, ss_send, ss_recv, first_send, first_recv, feed_send, feed_recv, again_send, again_recv,
    f_send, f_recv, b_send, b_recv, gp_send, gp_recv, ap_send, ap_recv, end_send, end_recv,
    late_send, late_recv, out_sem,
):
    width = half // CHUNKS
    inv_width = 1.0 / math.sqrt(D)
    inv_rank = BRANCH_SCALE / math.sqrt(RANK)
    s = lax.axis_index("pipe")
    dp = lax.axis_index("dp")
    c = lax.axis_index("mp")
    peer = 1 - c
    x = dp // 2
    yh = dp % 2
    x0 = x % 2
    x1 = x // 2
    x_one = (x + 1 - 2 * x0) * 2 + yh
    x_three = (3 - x) * 2 + yh
    y_other = x * 2 + 1 - yh
    is_first = s == 0
    is_last = s == sections - 1
    lag = 2 * sections - 1 - 2 * s
    late_section = lag < TICKS

    def remote(src, dst, send, recv, **where):
        return pltpu.make_async_remote_copy(
            src_ref=src, dst_ref=dst, send_sem=send, recv_sem=recv,
            device_id=where, device_id_type=MESH,
        )

    def landed(ref, sem):
        pltpu.make_async_copy(ref, ref, sem).wait()

    loads = [
        (fin, first.at[0, c]), (bin_, first.at[1, c]), (sq, ss.at[c]), (ex, ee.at[c]),
        (stash, st), (lsq, late.at[0]), (lex, late.at[1]),
    ]
    loads = [pltpu.make_async_copy(a, b, load_sem.at[i]) for i, (a, b) in enumerate(loads)]
    for load in loads:
        load.start()

    tick_of = s // 4
    feed_core = (s % 4) // 2
    feed_slot = c * 2 + s % 2
    own_feed = [is_first & (feed_core == c), is_last & (feed_core == c)]

    barrier = pltpu.get_barrier_semaphore()

    def hello(**where):
        pl.semaphore_signal(barrier, inc=1, device_id=where, device_id_type=MESH)

    hello(mp=peer)
    hello(dp=x_one)
    hello(dp=x_three)
    hello(dp=y_other)

    @pl.when(s > 0)
    def _():
        hello(pipe=s - 1)

    @pl.when(s < sections - 1)
    def _():
        hello(pipe=s + 1)

    for at_end in (is_first, is_last):
        @pl.when(at_end)
        def _():
            def greet(i, _):
                who = (i // 4) * 4 + 2 * c + (i // 2) % 2
                core = i % 2

                @pl.when((who != s) | (core != c))
                def _():
                    hello(pipe=who, mp=core)

                return 0

            lax.fori_loop(0, 4 * TICKS, greet, 0)

    expected = (
        4 + (s > 0).astype(jnp.int32) + (s < sections - 1).astype(jnp.int32)
        + 1 - own_feed[0].astype(jnp.int32) + 1 - own_feed[1].astype(jnp.int32)
    )
    pl.semaphore_wait(barrier, expected)

    firsts = [
        remote(src, first.at[i, c], first_send.at[i], first_recv.at[i], mp=peer)
        for i, src in enumerate((fin, bin_))
    ]
    weights = [
        remote(src, dst.at[c], ss_send.at[i], ss_recv.at[i], mp=peer)
        for i, (src, dst) in enumerate(((sq, ss), (ex, ee)))
    ]
    for copy in firsts + weights:
        copy.start()

    for k, (src, end) in enumerate(((act, 0), (cot, sections - 1))):
        @pl.when(own_feed[k])
        def _():
            pltpu.make_async_copy(
                src, feed.at[tick_of, feed_slot], feed_recv.at[tick_of, feed_slot]
            ).start()

        @pl.when(jnp.logical_not(own_feed[k]))
        def _():
            remote(
                src, feed.at[tick_of, feed_slot], feed_send.at[k],
                feed_recv.at[tick_of, feed_slot], pipe=end, mp=feed_core,
            ).start()

    b1 = (x0 + x1 - 2 * x0 * x1, x1)
    b2 = (x1, x0)
    near = (x_one, x_three)
    far = (x_three, x_one)
    sources = (lsq, lex)

    def rows(start, size):
        return pl.ds(pl.multiple_of(start, size), size)

    def late_copy(stage, h):
        sems = late_send.at[stage, h], late_recv.at[stage, h]
        if stage == 0:
            return remote(
                sources[h].at[rows(32 * (1 - b1[h]), 32)], r1.at[h], *sems, dp=near[h])
        if stage == 1:
            return remote(p1.at[h], r2.at[h], *sems, dp=far[h])
        if stage == 2:
            return remote(p2.at[h], ry.at[h], *sems, dp=y_other)
        if stage == 3:
            block = new.at[h, rows(32 * b1[h] + 16 * b2[h], 16)]
            return remote(block, block, *sems, dp=far[h])
        block = new.at[h, rows(32 * b1[h], 32)]
        return remote(block, block, *sems, dp=near[h])

    def late_landed(stage, h):
        if stage == 0:
            ref = r1.at[h]
        elif stage == 1:
            ref = r2.at[h]
        elif stage == 2:
            ref = ry.at[h]
        elif stage == 3:
            ref = new.at[h, rows(32 * b1[h] + 16 * (1 - b2[h]), 16)]
        else:
            ref = new.at[h, rows(32 * (1 - b1[h]), 32)]
        landed(ref, late_recv.at[stage, h])

    def late_step(stage, h):
        late_landed(stage, h)
        keep = rows(32 * b1[h] + 16 * b2[h], 16)
        give = rows(32 * b1[h] + 16 * (1 - b2[h]), 16)
        if stage == 0:
            p1[h] = (
                late[h, give, :].astype(F32) + r1[h, rows(16 * (1 - b2[h]), 16), :].astype(F32)
            ).astype(BF16)
        elif stage == 1:
            p2[h] = (
                late[h, keep, :].astype(F32) + r1[h, rows(16 * b2[h], 16), :].astype(F32)
                + r2[h].astype(F32)
            ).astype(BF16)
        elif stage == 2:
            total = p2[h].astype(F32) + ry[h].astype(F32)
            old = (ss, ee)[h][c, keep, :].astype(F32)
            new[h, keep, :] = (old - STEP_RATE * total / replicas).astype(BF16)
        if stage < 4:
            late_copy(stage + 1, h).start()

    for h in range(2):
        late_copy(0, h).start()

    for i in (2, 4):
        loads[i].wait()
    own_squeeze = ss[c]
    again[...] = rows_by_rows(st[...], jnp.concatenate([own_squeeze, own_squeeze], axis=0))
    again_copy = remote(again, again_peer, again_send, again_recv, mp=peer)
    again_copy.start()
    hg[...] = jnp.zeros_like(hg)
    rg[...] = jnp.zeros_like(rg)

    def crossed(w0, w1):
        w0 = w0.astype(F32)
        w1 = w1.astype(F32)
        low = jnp.concatenate([w0[:8], w1[:8]], axis=0)
        high = jnp.concatenate([w0[8:], w1[8:]], axis=0)
        return jnp.where(c == 0, low, high).astype(BF16)

    loads[0].wait()
    loads[1].wait()
    for i, (dst, at_end) in enumerate(((a_in, is_first), (g_in, is_last))):
        landed(first.at[i, peer], first_recv.at[i])
        for k in range(CHUNKS):
            cols = pl.ds(k * width, width)
            dst[0, k] = crossed(first[i, 0, :, cols], first[i, 1, :, cols])
    loads[3].wait()
    loads[5].wait()
    loads[6].wait()
    landed(ss.at[peer], ss_recv.at[0])
    landed(ee.at[peer], ss_recv.at[1])
    again_copy.wait()
    again[...] = (again[...] + again_peer[...]) * inv_width

    own_block = (lax.broadcasted_iota(jnp.int32, (ROWS, 2 * RANK), 0) < 8) == (
        lax.broadcasted_iota(jnp.int32, (ROWS, 2 * RANK), 1) < RANK
    )
    low_lanes = lax.broadcasted_iota(jnp.int32, (8, 2 * RANK), 1) < RANK

    def stacked(ref, k):
        return ref[:, :, pl.ds(k * width, width)].reshape(2 * RANK, width)

    def both(v):
        swapped = jnp.concatenate([v[8:], v[:8]], axis=0)
        return v + pltpu.roll(swapped, RANK, 1)

    def from_feed(tick, dst):
        for j in range(4):
            landed(feed.at[tick, j], feed_recv.at[tick, j])
        for j in range(4):
            feed_rows[pl.ds(4 * j, 4), :] = feed[tick, j].astype(F32)
        for k in range(CHUNKS):
            dst[tick, k] = feed_rows[:, pl.ds(k * width, width)].astype(BF16)

    def forward_copy(tick, k):
        return remote(
            a_out.at[tick, k], a_in.at[tick + 1, k], f_send.at[tick, k], f_recv.at[tick + 1, k],
            pipe=s + 1)

    def backward_copy(tick, k):
        return remote(
            g_out.at[tick, k], g_in.at[tick + 1, k], b_send.at[tick, k], b_recv.at[tick + 1, k],
            pipe=s - 1)

    def peer_copy(tick, src, dst, send, recv):
        return remote(src.at[tick], dst.at[tick], send.at[tick], recv.at[tick], mp=peer)

    def tick_body(tick, _):
        mine = pl.ds(pl.multiple_of(tick * ROWS + 8 * c, 8), 8)
        seen = again[mine, :]
        slope = gelu_slope(seen)
        rg[mine, :] = gelu(seen).astype(BF16).astype(F32)
        slope = jnp.concatenate([slope, slope], axis=0)

        @pl.when(is_first)
        def _():
            from_feed(tick, a_in)

        hidden = jnp.zeros((ROWS, 2 * RANK), F32)
        for k in range(CHUNKS):
            @pl.when(jnp.logical_not(is_first) & (tick > 0))
            def _():
                landed(a_in.at[tick, k], f_recv.at[tick, k])

            hidden = hidden + rows_by_rows(a_in[tick, k], stacked(ss, k))
        hidden = both(hidden) * inv_width
        gated = jnp.where(own_block, gelu(hidden), 0.0).astype(BF16)
        for k in range(CHUNKS):
            a_out[tick, k] = (
                a_in[tick, k].astype(F32) + times(gated, stacked(ee, k)) * inv_rank
            ).astype(BF16)

            @pl.when((tick < TICKS - 1) & (s < sections - 1))
            def _():
                forward_copy(tick, k).start()

        @pl.when(is_last)
        def _():
            from_feed(tick, g_in)

        gate_grad = jnp.zeros((ROWS, 2 * RANK), F32)
        for k in range(CHUNKS):
            @pl.when(jnp.logical_not(is_last) & (tick > 0))
            def _():
                landed(g_in.at[tick, k], b_recv.at[tick, k])

            gate_grad = gate_grad + rows_by_rows(g_in[tick, k], stacked(ee, k))
        gate_grad = both(gate_grad) * inv_rank
        hidden_grad = jnp.where(own_block, gate_grad * slope, 0.0).astype(BF16)
        for k in range(CHUNKS):
            g_out[tick, k] = (
                g_in[tick, k].astype(F32) + times(hidden_grad, stacked(ss, k)) * inv_width
            ).astype(BF16)

            @pl.when((tick < TICKS - 1) & (s > 0))
            def _():
                backward_copy(tick, k).start()

        hg[mine, :] = hidden_grad.astype(F32)[:8]
        peer_copy(tick, g_in, g_peer, gp_send, gp_recv).start()

        @pl.when(late_section)
        def _():
            peer_copy(tick, a_in, a_peer, ap_send, ap_recv).start()

            @pl.when(tick + lag < TICKS)
            def _():
                later = pl.ds(pl.multiple_of((tick + lag) * ROWS + 8 * c, 8), 8)
                again[later, :] = jnp.where(low_lanes, hidden[:8], hidden[8:])

        for stage, at in enumerate((1, 2, 5, 6)):
            @pl.when(tick == at)
            def _():
                for h in range(2):
                    late_step(stage, h)

        return 0

    lax.fori_loop(0, TICKS, tick_body, 0)

    ends = [
        remote(src, dst, end_send.at[i], end_recv.at[i], mp=peer)
        for i, (src, dst) in enumerate((
            (hg, hg_peer), (rg, rg_peer),
            (a_out.at[TICKS - 1], carry_peer.at[0]), (g_out.at[TICKS - 1], carry_peer.at[1]),
        ))
    ]
    for copy in ends:
        copy.start()
    ends[0].wait()
    ends[1].wait()

    def swapped_rows(v):
        v = v.reshape(TICKS, 2, 8, 2 * RANK)
        return jnp.concatenate([v[:, 1:], v[:, :1]], axis=1).reshape(TICKS * ROWS, 2 * RANK)

    def as_left(v):
        return jnp.transpose(v)[:RANK].astype(BF16)

    def all_ticks(ref, k):
        return ref[:, k].reshape(TICKS * ROWS, width)

    total_hg = hg[...] + hg_peer[...]
    row = lax.broadcasted_iota(jnp.int32, (TICKS * ROWS, 2 * RANK), 0)
    left = as_left(jnp.where(row < lag * ROWS, total_hg, 0.0))
    for k in range(CHUNKS):
        cols = pl.ds(k * width, width)
        grads[0, :, cols] = times(left, st[:, cols]) * inv_width

    @pl.when(late_section)
    def _():
        for tick in range(TICKS):
            peer_copy(tick, a_in, a_peer, ap_send, ap_recv).wait()
        moved = []
        for ref, swap in ((hg, False), (hg_peer, True)):
            pieces = []
            for tick in range(TICKS):
                source = jnp.minimum(tick + lag, TICKS - 1)
                piece = ref[pl.ds(pl.multiple_of(source * ROWS, ROWS), ROWS), :]
                if swap:
                    piece = jnp.concatenate([piece[8:], piece[:8]], axis=0)
                pieces.append(jnp.where(tick + lag < TICKS, piece, 0.0))
            moved.append(as_left(jnp.concatenate(pieces, axis=0)))
        for k in range(CHUNKS):
            cols = pl.ds(k * width, width)
            grads[0, :, cols] = grads[0, :, cols] + inv_width * (
                times(moved[0], all_ticks(a_in, k)) + times(moved[1], all_ticks(a_peer, k))
            )

    for tick in range(TICKS):
        peer_copy(tick, g_in, g_peer, gp_send, gp_recv).wait()
    own_left = as_left(rg[...])
    peer_left = as_left(swapped_rows(rg_peer[...]))
    for k in range(CHUNKS):
        cols = pl.ds(k * width, width)
        grads[1, :, cols] = inv_rank * (
            times(own_left, all_ticks(g_in, k)) + times(peer_left, all_ticks(g_peer, k))
        )
    gsq[...] = grads[0].astype(BF16)
    gex[...] = grads[1].astype(BF16)

    ends[2].wait()
    ends[3].wait()
    for i, (src, out) in enumerate(((a_out, fco), (g_out, bco))):
        for k in range(CHUNKS):
            mine = src[TICKS - 1, k].astype(F32)
            other = carry_peer[i, k].astype(F32)
            out[:, pl.ds(k * width, width)] = crossed(
                jnp.where(c == 0, mine, other), jnp.where(c == 0, other, mine))

    for h in range(2):
        late_landed(4, h)
    nsq[...] = new[0]
    nex[...] = new[1]

    for copy in firsts + weights:
        copy.wait_send()
    for k, (src, end) in enumerate(((act, 0), (cot, sections - 1))):
        @pl.when(jnp.logical_not(own_feed[k]))
        def _():
            remote(
                src, feed.at[tick_of, feed_slot], feed_send.at[k],
                feed_recv.at[tick_of, feed_slot], pipe=end, mp=feed_core,
            ).wait_send()
    for stage in range(5):
        for h in range(2):
            late_copy(stage, h).wait_send()

    def sent(tick, _):
        for k in range(CHUNKS):
            @pl.when(s < sections - 1)
            def _():
                forward_copy(tick, k).wait_send()

            @pl.when(s > 0)
            def _():
                backward_copy(tick, k).wait_send()

        return 0

    lax.fori_loop(0, TICKS - 1, sent, 0)


def shards(
    activations, cotangent, squeeze_old, expand_old, squeeze_late, expand_late,
    stash_inputs, forward_in, backward_in,
):
    sections = lax.axis_size("pipe")
    replicas = lax.axis_size("dp")
    half = squeeze_old.shape[1]
    width = half // CHUNKS
    vmem = pltpu.VMEM
    dma = pltpu.SemaphoreType.DMA
    ticked = vmem((TICKS, CHUNKS, ROWS, width), BF16)
    small = vmem((TICKS * ROWS, 2 * RANK), F32)
    any_spec = pl.BlockSpec(memory_space=pl.ANY)
    vmem_spec = pl.BlockSpec(memory_space=pltpu.VMEM)
    outs = pl.pallas_call(
        functools.partial(window, sections, replicas, half),
        out_shape=[jax.ShapeDtypeStruct((RANK, half), BF16)] * 4
        + [jax.ShapeDtypeStruct((ROWS, half), BF16)] * 2,
        in_specs=[any_spec] * 9,
        out_specs=[vmem_spec] * 6,
        scratch_shapes=[
            vmem((2, RANK, half), BF16),
            vmem((2, RANK, half), BF16),
            vmem((TICKS * ROWS, half), BF16),
            vmem((2, 2, ROWS, half), BF16),
            ticked, ticked, ticked, ticked, ticked, ticked,
            vmem((2, CHUNKS, ROWS, width), BF16),
            vmem((TICKS, 4, 4, half), BF16),
            vmem((ROWS, half), F32),
            small, small, small, small, small, small,
            vmem((2, RANK, half), BF16),
            vmem((2, 32, half), BF16),
            vmem((2, 16, half), BF16),
            vmem((2, 16, half), BF16),
            vmem((2, 16, half), BF16),
            vmem((2, 16, half), BF16),
            vmem((2, RANK, half), BF16),
            vmem((2, RANK, half), F32),
            vmem((8, 128), F32),
            dma((7,)),
            dma((2,)), dma((2,)),
            dma((2,)), dma((2,)),
            dma((2,)), dma((TICKS, 4)),
            dma, dma,
            dma((TICKS, CHUNKS)), dma((TICKS, CHUNKS)),
            dma((TICKS, CHUNKS)), dma((TICKS, CHUNKS)),
            dma((TICKS,)), dma((TICKS,)), dma((TICKS,)), dma((TICKS,)),
            dma((4,)), dma((4,)),
            dma((5, 2)), dma((5, 2)),
            dma((6,)),
        ],
        compiler_params=pltpu.CompilerParams(
            collective_id=0, has_side_effects=True, vmem_limit_bytes=48 * 1024 * 1024
        ),
        name="window",
    )(
        activations[0], cotangent[0], squeeze_old[0].T, expand_old[0],
        squeeze_late[0, 0].T, expand_late[0, 0], stash_inputs[0, 0].reshape(TICKS * ROWS, half),
        forward_in[0, 0], backward_in[0, 0],
    )
    nsq, nex, gsq, gex, fco, bco = outs
    return (
        nsq.T[None], nex[None], gsq.T[None, None], gex[None, None],
        fco[None, None], bco[None, None],
    )


def solution(mesh):
    placed = (
        P("dp", "pipe", "mp"),
        P("dp", "pipe", "mp"),
        P("pipe", "mp", None),
        P("pipe", None, "mp"),
        P("dp", "pipe", "mp", None),
        P("dp", "pipe", None, "mp"),
        P("dp", "pipe", None, None, "mp"),
        P("dp", "pipe", None, "mp"),
        P("dp", "pipe", None, "mp"),
    )
    return jax.shard_map(
        shards,
        mesh=mesh,
        in_specs=placed,
        out_specs=(
            P("pipe", "mp", None),
            P("pipe", None, "mp"),
            P("dp", "pipe", "mp", None),
            P("dp", "pipe", None, "mp"),
            P("dp", "pipe", None, "mp"),
            P("dp", "pipe", None, "mp"),
        ),
        check_vma=False,
    )
```

```python
import functools
import math

import jax
import jax.numpy as jnp
from jax import lax
from jax.experimental import pallas as pl
from jax.experimental.pallas import tpu as pltpu
from jax.sharding import PartitionSpec as P

D = 7168
RANK = 64
TICKS = 8
ROWS = 16
BRANCH_SCALE = 0.25
STEP_RATE = 0.5
GROUPS = 2
GROUP = 8
LATE_TICKS = ((1, 1), (2, 4), (3, 5))

F32 = jnp.float32
BF16 = jnp.bfloat16
MESH = pl.DeviceIdType.MESH
GELU_A = math.sqrt(2.0 / math.pi)
GELU_B = 0.044715


def gelu(v):
    return 0.5 * v * (1.0 + jnp.tanh(GELU_A * (v + GELU_B * (v * v * v))))


def gelu_slope(v):
    t = jnp.tanh(GELU_A * (v + GELU_B * (v * v * v)))
    inner = GELU_A * (1.0 + 3.0 * GELU_B * (v * v))
    return 0.5 * (1.0 + t) + 0.5 * v * ((1.0 - t * t) * inner)


def rows_by_rows(left, right):
    return lax.dot_general(left, right, (((1,), (1,)), ((), ())), preferred_element_type=F32)


def times(left, right):
    return jnp.dot(left, right, preferred_element_type=F32)


def window(
    sections, replicas, half,
    act, cot, sq, ex, lsq, lex, stash, fin, bin_,
    nsq, nex, gsq, gex, fco, bco,
    ss, ee, st, first, s_cols, e_cols, a_in, g_in, a_out, g_out, a_peer, g_peer, carry_peer,
    feed, feed_rows, again, again_peer, hg, rg, hg_peer, rg_peer, late, r1, p1, r2, p2, ry, new,
    grads, grads_out, carry,
    load_sem, ss_send, ss_recv, first_send, first_recv, feed_send, feed_recv, again_send, again_recv,
    f_send, f_recv, b_send, b_recv, gp_send, gp_recv, ap_send, ap_recv, end_send, end_recv,
    late_send, late_recv, out_sem,
):
    inv_width = 1.0 / math.sqrt(D)
    inv_rank = BRANCH_SCALE / math.sqrt(RANK)
    s = lax.axis_index("pipe")
    dp = lax.axis_index("dp")
    c = lax.axis_index("mp")
    peer = 1 - c
    x = dp // 2
    yh = dp % 2
    x0 = x % 2
    x1 = x // 2
    x_one = (x + 1 - 2 * x0) * 2 + yh
    x_three = (3 - x) * 2 + yh
    y_other = x * 2 + 1 - yh
    is_first = s == 0
    is_last = s == sections - 1
    lag = 2 * sections - 1 - 2 * s
    late_section = lag < TICKS

    def remote(src, dst, send, recv, **where):
        return pltpu.make_async_remote_copy(
            src_ref=src, dst_ref=dst, send_sem=send, recv_sem=recv,
            device_id=where, device_id_type=MESH,
        )

    def landed(ref, sem):
        pltpu.make_async_copy(ref, ref, sem).wait()

    loads = [
        (fin, first.at[0, c]), (bin_, first.at[1, c]), (sq, ss.at[c]), (ex, ee.at[c]),
        (stash, st), (lsq, late.at[0]), (lex, late.at[1]),
    ]
    loads = [pltpu.make_async_copy(a, b, load_sem.at[i]) for i, (a, b) in enumerate(loads)]
    for load in loads:
        load.start()

    feed_tick = s // 4
    feed_group = (s % 4) // 2
    feed_core = s % 2
    own_feed = [is_first & (feed_core == c), is_last & (feed_core == c)]

    barrier = pltpu.get_barrier_semaphore()

    def hello(**where):
        pl.semaphore_signal(barrier, inc=1, device_id=where, device_id_type=MESH)

    hello(mp=peer)
    hello(dp=x_one)
    hello(dp=x_three)
    hello(dp=y_other)

    @pl.when(s > 0)
    def _():
        hello(pipe=s - 1)

    @pl.when(s < sections - 1)
    def _():
        hello(pipe=s + 1)

    for at_end in (is_first, is_last):
        @pl.when(at_end)
        def _():
            def greet(i, _):
                who = (i // 2) * 2 + c
                core = i % 2

                @pl.when((who != s) | (core != c))
                def _():
                    hello(pipe=who, mp=core)

                return 0

            lax.fori_loop(0, sections, greet, 0)

    expected = (
        4 + (s > 0).astype(jnp.int32) + (s < sections - 1).astype(jnp.int32)
        + 1 - own_feed[0].astype(jnp.int32) + 1 - own_feed[1].astype(jnp.int32)
    )
    pl.semaphore_wait(barrier, expected)

    firsts = [
        remote(src, first.at[i, c], first_send.at[i], first_recv.at[i], mp=peer)
        for i, src in enumerate((fin, bin_))
    ]
    weights = [
        remote(src, dst.at[c], ss_send.at[i], ss_recv.at[i], mp=peer)
        for i, (src, dst) in enumerate(((sq, ss), (ex, ee)))
    ]
    for copy in firsts + weights:
        copy.start()

    def send_feed():
        for k, (src, end) in enumerate(((act, 0), (cot, sections - 1))):
            slot = feed.at[feed_tick, feed_group, c]
            sem = feed_recv.at[feed_tick, feed_group, c]

            @pl.when(own_feed[k])
            def _():
                pltpu.make_async_copy(src, slot, sem).start()

            @pl.when(jnp.logical_not(own_feed[k]))
            def _():
                remote(src, slot, feed_send.at[k], sem, pipe=end, mp=feed_core).start()

    pl.when(feed_tick < 2)(send_feed)

    b1 = (x0 + x1 - 2 * x0 * x1, x1)
    b2 = (x1, x0)
    near = (x_one, x_three)
    far = (x_three, x_one)
    sources = (lsq, lex)

    def rows(start, size):
        return pl.ds(pl.multiple_of(start, size), size)

    def late_copy(stage, h):
        sems = late_send.at[stage, h], late_recv.at[stage, h]
        if stage == 0:
            return remote(
                sources[h].at[rows(32 * (1 - b1[h]), 32)], r1.at[h], *sems, dp=near[h])
        if stage == 1:
            return remote(p1.at[h], r2.at[h], *sems, dp=far[h])
        if stage == 2:
            return remote(p2.at[h], ry.at[h], *sems, dp=y_other)
        if stage == 3:
            block = new.at[h, rows(32 * b1[h] + 16 * b2[h], 16)]
            return remote(block, block, *sems, dp=far[h])
        block = new.at[h, rows(32 * b1[h], 32)]
        return remote(block, block, *sems, dp=near[h])

    def late_landed(stage, h):
        if stage == 0:
            ref = r1.at[h]
        elif stage == 1:
            ref = r2.at[h]
        elif stage == 2:
            ref = ry.at[h]
        elif stage == 3:
            ref = new.at[h, rows(32 * b1[h] + 16 * (1 - b2[h]), 16)]
        else:
            ref = new.at[h, rows(32 * (1 - b1[h]), 32)]
        landed(ref, late_recv.at[stage, h])

    def late_step(stage, h):
        late_landed(stage, h)
        keep = rows(32 * b1[h] + 16 * b2[h], 16)
        give = rows(32 * b1[h] + 16 * (1 - b2[h]), 16)
        if stage == 0:
            p1[h] = (
                late[h, give, :].astype(F32) + r1[h, rows(16 * (1 - b2[h]), 16), :].astype(F32)
            ).astype(BF16)
        elif stage == 1:
            p2[h] = (
                late[h, keep, :].astype(F32) + r1[h, rows(16 * b2[h], 16), :].astype(F32)
                + r2[h].astype(F32)
            ).astype(BF16)
        elif stage == 2:
            total = p2[h].astype(F32) + ry[h].astype(F32)
            old = (ss, ee)[h][c, keep, :].astype(F32)
            new[h, keep, :] = (old - STEP_RATE * total / replicas).astype(BF16)
        if stage < 4:
            late_copy(stage + 1, h).start()

    for h in range(2):
        late_copy(0, h).start()

    for i in (2, 4):
        loads[i].wait()
    own_squeeze = ss[c]
    again[...] = rows_by_rows(st[...], jnp.concatenate([own_squeeze, own_squeeze], axis=0))
    again_copy = remote(again, again_peer, again_send, again_recv, mp=peer)
    again_copy.start()
    hg[...] = jnp.zeros_like(hg)
    rg[...] = jnp.zeros_like(rg)

    upper = lax.broadcasted_iota(jnp.int32, (GROUP, 2 * RANK), 0) < 4
    own_block = upper == (lax.broadcasted_iota(jnp.int32, (GROUP, 2 * RANK), 1) < RANK)
    own_rows = upper == (c == 0)
    upper_wide = lax.broadcasted_iota(jnp.int32, (GROUP, half), 0) < 4

    def crossed(w0, w1):
        w0 = w0.astype(F32)
        w1 = w1.astype(F32)
        low = jnp.where(upper_wide, w0, pltpu.roll(w1, 4, 0))
        high = jnp.where(upper_wide, pltpu.roll(w0, 4, 0), w1)
        return jnp.where(c == 0, low, high)

    loads[0].wait()
    loads[1].wait()
    for i, dst in enumerate((a_in, g_in)):
        landed(first.at[i, peer], first_recv.at[i])
        w0 = first[i, 0].astype(F32)
        w1 = first[i, 1].astype(F32)
        for g in range(GROUPS):
            mine = slice(GROUP * g, GROUP * (g + 1))
            dst[0, g] = crossed(w0[mine], w1[mine]).astype(BF16)
    loads[3].wait()
    loads[5].wait()
    loads[6].wait()
    landed(ss.at[peer], ss_recv.at[0])
    landed(ee.at[peer], ss_recv.at[1])

    def stacked(ref):
        return ref[...].reshape(2 * RANK, half)

    def both(v):
        return v + pltpu.roll(pltpu.roll(v, 4, 0), RANK, 1)

    def spread(v):
        return jnp.where(own_block, v, pltpu.roll(v, RANK, 1))

    def from_feed(tick, g, dst):
        for h in range(2):
            landed(feed.at[tick, g, h], feed_recv.at[tick, g, h])
        for h in range(2):
            feed_rows[pl.ds(4 * h, 4), :] = feed[tick, g, h].astype(F32)
        dst[tick, g] = feed_rows[pl.ds(0, GROUP), :].astype(BF16)

    def forward_copy(tick, g):
        return remote(
            a_out.at[tick, g], a_in.at[tick + 1, g], f_send.at[tick, g], f_recv.at[tick + 1, g],
            pipe=s + 1)

    def backward_copy(tick, g):
        return remote(
            g_out.at[tick, g], g_in.at[tick + 1, g], b_send.at[tick, g], b_recv.at[tick + 1, g],
            pipe=s - 1)

    def peer_copy(tick, src, dst, send, recv):
        return remote(src.at[tick], dst.at[tick], send.at[tick], recv.at[tick], mp=peer)

    def tile(tick, g):
        return pl.ds(pl.multiple_of(tick * ROWS + GROUP * g, GROUP), GROUP)

    def forward(tick, g, project):
        hidden = both(project(a_in[tick, g], ss, s_cols)) * inv_width
        gated = jnp.where(own_block, gelu(hidden), 0.0).astype(BF16)
        a_out[tick, g] = (
            a_in[tick, g].astype(F32) + times(gated, stacked(ee)) * inv_rank
        ).astype(BF16)

        @pl.when((tick < TICKS - 1) & (s < sections - 1))
        def _():
            forward_copy(tick, g).start()

        return hidden

    def keep_hidden(tick, g, hidden):
        @pl.when(tick + lag < TICKS)
        def _():
            again[tile(tick + lag, g), :] = spread(hidden)

    def backward(tick, g, slope, project):
        gate_grad = both(project(g_in[tick, g], ee, e_cols)) * inv_rank
        hidden_grad = jnp.where(own_block, gate_grad * slope, 0.0).astype(BF16)
        g_out[tick, g] = (
            g_in[tick, g].astype(F32) + times(hidden_grad, stacked(ss)) * inv_width
        ).astype(BF16)

        @pl.when((tick < TICKS - 1) & (s > 0))
        def _():
            backward_copy(tick, g).start()

        hg[tile(tick, g), :] = jnp.where(own_rows, spread(hidden_grad.astype(F32)), 0.0)

    def recomputed(tick, g):
        seen = again[tile(tick, g), :]
        seen = jnp.where(own_rows, seen, pltpu.roll(seen, 4, 0))
        rg[tile(tick, g), :] = jnp.where(own_rows, gelu(seen).astype(BF16).astype(F32), 0.0)
        return gelu_slope(seen)

    def after(tick):
        peer_copy(tick, g_in, g_peer, gp_send, gp_recv).start()

        @pl.when(late_section)
        def _():
            peer_copy(tick, a_in, a_peer, ap_send, ap_recv).start()

        @pl.when(feed_tick == tick + 2)
        def _():
            send_feed()

    def from_weights(v, ref, _):
        return rows_by_rows(v, stacked(ref))

    def from_columns(v, _, ref):
        return times(v, ref[...])

    hidden = [None] * GROUPS
    for g in range(GROUPS):
        @pl.when(is_first)
        def _():
            from_feed(0, g, a_in)

        hidden[g] = forward(0, g, from_weights)
    again_copy.wait()
    again[...] = (again[...] + again_peer[...]) * inv_width
    for g in range(GROUPS):
        keep_hidden(0, g, hidden[g])

        @pl.when(is_last)
        def _():
            from_feed(0, g, g_in)

        backward(0, g, recomputed(0, g), from_weights)
    after(0)
    for k in range(7):
        cols = pl.ds(k * (half // 7), half // 7)
        s_cols[cols, :] = jnp.transpose(ss[:, :, cols].reshape(2 * RANK, half // 7))
        e_cols[cols, :] = jnp.transpose(ee[:, :, cols].reshape(2 * RANK, half // 7))
    for h in range(2):
        late_step(0, h)

    def tick_body(tick, _):
        slopes = [recomputed(tick, g) for g in range(GROUPS)]
        for g in range(GROUPS):
            @pl.when(is_first)
            def _():
                from_feed(tick, g, a_in)

            @pl.when(jnp.logical_not(is_first))
            def _():
                landed(a_in.at[tick, g], f_recv.at[tick, g])

            keep_hidden(tick, g, forward(tick, g, from_columns))

            @pl.when(is_last)
            def _():
                from_feed(tick, g, g_in)

            @pl.when(jnp.logical_not(is_last))
            def _():
                landed(g_in.at[tick, g], b_recv.at[tick, g])

            backward(tick, g, slopes[g], from_columns)

        after(tick)
        for stage, at in LATE_TICKS:
            @pl.when(tick == at)
            def _():
                for h in range(2):
                    late_step(stage, h)

        return 0

    lax.fori_loop(1, TICKS, tick_body, 0)

    ends = [
        remote(src, dst, end_send.at[i], end_recv.at[i], mp=peer)
        for i, (src, dst) in enumerate((
            (hg, hg_peer), (rg, rg_peer),
            (a_out.at[TICKS - 1], carry_peer.at[0]), (g_out.at[TICKS - 1], carry_peer.at[1]),
        ))
    ]
    for copy in ends:
        copy.start()
    outs = []

    def put(src, dst):
        copy = pltpu.make_async_copy(src, dst, out_sem.at[len(outs)])
        copy.start()
        outs.append(copy)

    ends[0].wait()
    ends[1].wait()

    def swapped_rows(v):
        v = v.reshape(-1, 2, 4, 2 * RANK)
        return jnp.concatenate([v[:, 1:], v[:, :1]], axis=1).reshape(-1, 2 * RANK)

    def as_left(v):
        return jnp.transpose(v)[:RANK].astype(BF16)

    def all_ticks(ref):
        return ref[...].reshape(TICKS * ROWS, half)

    for tick in range(TICKS):
        peer_copy(tick, g_in, g_peer, gp_send, gp_recv).wait()
    grads_out[1] = (inv_rank * (
        times(as_left(rg[...]), all_ticks(g_in))
        + times(as_left(swapped_rows(rg_peer[...])), all_ticks(g_peer))
    )).astype(BF16)
    put(grads_out.at[1], gex)

    total_hg = hg[...] + hg_peer[...]
    row = lax.broadcasted_iota(jnp.int32, (TICKS * ROWS, 2 * RANK), 0)
    left = as_left(jnp.where(row < lag * ROWS, total_hg, 0.0))
    grads[...] = times(left, st[...])

    @pl.when(late_section)
    def _():
        for tick in range(TICKS):
            peer_copy(tick, a_in, a_peer, ap_send, ap_recv).wait()
        moved = []
        for ref, swap in ((hg, False), (hg_peer, True)):
            pieces = []
            for tick in range(TICKS):
                source = jnp.minimum(tick + lag, TICKS - 1)
                piece = ref[pl.ds(pl.multiple_of(source * ROWS, ROWS), ROWS), :]
                if swap:
                    piece = swapped_rows(piece)
                pieces.append(jnp.where(tick + lag < TICKS, piece, 0.0))
            moved.append(as_left(jnp.concatenate(pieces, axis=0)))
        grads[...] = (
            grads[...] + times(moved[0], all_ticks(a_in)) + times(moved[1], all_ticks(a_peer))
        )

    grads_out[0] = (inv_width * grads[...]).astype(BF16)
    put(grads_out.at[0], gsq)

    ends[2].wait()
    ends[3].wait()
    for i, (src, out) in enumerate(((a_out, fco), (g_out, bco))):
        for g in range(GROUPS):
            mine = src[TICKS - 1, g].astype(F32)
            other = carry_peer[i, g].astype(F32)
            feed_rows[pl.ds(GROUP * g, GROUP), :] = crossed(
                jnp.where(c == 0, mine, other), jnp.where(c == 0, other, mine))
        carry[i] = feed_rows[...].astype(BF16)
        put(carry.at[i], out)

    for h, out in enumerate((nsq, nex)):
        late_landed(4, h)
        put(new.at[h], out)

    for copy in firsts + weights:
        copy.wait_send()
    for k, (src, end) in enumerate(((act, 0), (cot, sections - 1))):
        @pl.when(jnp.logical_not(own_feed[k]))
        def _():
            remote(
                src, feed.at[feed_tick, feed_group, c], feed_send.at[k],
                feed_recv.at[feed_tick, feed_group, c], pipe=end, mp=feed_core,
            ).wait_send()
    for stage in range(5):
        for h in range(2):
            late_copy(stage, h).wait_send()

    def sent(tick, _):
        for g in range(GROUPS):
            @pl.when(s < sections - 1)
            def _():
                forward_copy(tick, g).wait_send()

            @pl.when(s > 0)
            def _():
                backward_copy(tick, g).wait_send()

        return 0

    lax.fori_loop(0, TICKS - 1, sent, 0)
    for copy in outs:
        copy.wait()


def put_out(*refs):
    sources, outs, held, sems = refs[:6], refs[6:12], refs[12:18], refs[18]
    ins = [pltpu.make_async_copy(a, b, sems.at[0, i]) for i, (a, b) in enumerate(zip(sources, held))]
    out = [pltpu.make_async_copy(a, b, sems.at[1, i]) for i, (a, b) in enumerate(zip(held, outs))]
    for copy in ins:
        copy.start()
    for first, second in zip(ins, out):
        first.wait()
        second.start()
    for copy in out:
        copy.wait()


def shards(
    activations, cotangent, squeeze_old, expand_old, squeeze_late, expand_late,
    stash_inputs, forward_in, backward_in,
):
    sections = lax.axis_size("pipe")
    replicas = lax.axis_size("dp")
    half = squeeze_old.shape[1]
    vmem = pltpu.VMEM
    dma = pltpu.SemaphoreType.DMA
    ticked = vmem((TICKS, GROUPS, GROUP, half), BF16)
    small = vmem((TICKS * ROWS, 2 * RANK), F32)
    hbm_spec = pl.BlockSpec(memory_space=pltpu.HBM)
    outs = pl.pallas_call(
        functools.partial(window, sections, replicas, half),
        out_shape=[jax.ShapeDtypeStruct((RANK, half), BF16)] * 4
        + [jax.ShapeDtypeStruct((ROWS, half), BF16)] * 2,
        in_specs=[hbm_spec] * 9,
        out_specs=[hbm_spec] * 6,
        scratch_shapes=[
            vmem((2, RANK, half), BF16),
            vmem((2, RANK, half), BF16),
            vmem((TICKS * ROWS, half), BF16),
            vmem((2, 2, ROWS, half), BF16),
            vmem((half, 2 * RANK), BF16),
            vmem((half, 2 * RANK), BF16),
            ticked, ticked, ticked, ticked, ticked, ticked,
            vmem((2, GROUPS, GROUP, half), BF16),
            vmem((TICKS, GROUPS, 2, 4, half), BF16),
            vmem((ROWS, half), F32),
            small, small, small, small, small, small,
            vmem((2, RANK, half), BF16),
            vmem((2, 32, half), BF16),
            vmem((2, 16, half), BF16),
            vmem((2, 16, half), BF16),
            vmem((2, 16, half), BF16),
            vmem((2, 16, half), BF16),
            vmem((2, RANK, half), BF16),
            vmem((RANK, half), F32),
            vmem((2, RANK, half), BF16),
            vmem((2, ROWS, half), BF16),
            dma((7,)),
            dma((2,)), dma((2,)),
            dma((2,)), dma((2,)),
            dma((2,)), dma((TICKS, GROUPS, 2)),
            dma, dma,
            dma((TICKS, GROUPS)), dma((TICKS, GROUPS)),
            dma((TICKS, GROUPS)), dma((TICKS, GROUPS)),
            dma((TICKS,)), dma((TICKS,)), dma((TICKS,)), dma((TICKS,)),
            dma((4,)), dma((4,)),
            dma((5, 2)), dma((5, 2)),
            dma((6,)),
        ],
        compiler_params=pltpu.CompilerParams(
            collective_id=0, has_side_effects=True, vmem_limit_bytes=62 * 1024 * 1024
        ),
        name="window",
    )(
        activations[0], cotangent[0], squeeze_old[0].T, expand_old[0],
        squeeze_late[0, 0].T, expand_late[0, 0], stash_inputs[0, 0].reshape(TICKS * ROWS, half),
        forward_in[0, 0], backward_in[0, 0],
    )
    nsq, nex, gsq, gex, fco, bco = pl.pallas_call(
        put_out,
        out_shape=[jax.ShapeDtypeStruct(out.shape, out.dtype) for out in outs],
        in_specs=[hbm_spec] * 6,
        out_specs=[hbm_spec] * 6,
        scratch_shapes=[vmem(out.shape, out.dtype) for out in outs] + [dma((2, 6))],
        compiler_params=pltpu.CompilerParams(vmem_limit_bytes=62 * 1024 * 1024),
        name="put_out",
    )(*outs)
    return (
        nsq.T[None], nex[None], gsq.T[None, None], gex[None, None],
        fco[None, None], bco[None, None],
    )


def solution(mesh):
    placed = (
        P("dp", "pipe", "mp"),
        P("dp", "pipe", "mp"),
        P("pipe", "mp", None),
        P("pipe", None, "mp"),
        P("dp", "pipe", "mp", None),
        P("dp", "pipe", None, "mp"),
        P("dp", "pipe", None, None, "mp"),
        P("dp", "pipe", None, "mp"),
        P("dp", "pipe", None, "mp"),
    )
    return jax.shard_map(
        shards,
        mesh=mesh,
        in_specs=placed,
        out_specs=(
            P("pipe", "mp", None),
            P("pipe", None, "mp"),
            P("dp", "pipe", "mp", None),
            P("dp", "pipe", None, "mp"),
            P("dp", "pipe", None, "mp"),
            P("dp", "pipe", None, "mp"),
        ),
        check_vma=False,
    )
```

```python
import functools
import math

import jax
import jax.numpy as jnp
from jax import lax
from jax.experimental import pallas as pl
from jax.experimental.pallas import tpu as pltpu
from jax.sharding import PartitionSpec as P

D = 7168
RANK = 64
TICKS = 8
ROWS = 16
BRANCH_SCALE = 0.25
STEP_RATE = 0.5
GROUPS = 2
GROUP = 8
SUM_TICK = 1
EXCHANGE_TICKS = ((1, 2), (3, 4))
RENEW_TICKS = (4, 6)

F32 = jnp.float32
BF16 = jnp.bfloat16
MESH = pl.DeviceIdType.MESH
GELU_A = math.sqrt(2.0 / math.pi)
GELU_B = 0.044715


def gelu(v):
    return 0.5 * v * (1.0 + jnp.tanh(GELU_A * (v + GELU_B * (v * v * v))))


def gelu_slope(v):
    t = jnp.tanh(GELU_A * (v + GELU_B * (v * v * v)))
    inner = GELU_A * (1.0 + 3.0 * GELU_B * (v * v))
    return 0.5 * (1.0 + t) + 0.5 * v * ((1.0 - t * t) * inner)


def rows_by_rows(left, right):
    return lax.dot_general(left, right, (((1,), (1,)), ((), ())), preferred_element_type=F32)


def times(left, right):
    return jnp.dot(left, right, preferred_element_type=F32)


def window(
    sections, replicas, half,
    act, cot, sq, ex, lsq, lex, stash, fin, bin_,
    nsq, nex, gsq, gex, fco, bco,
    w, st, first, cols, x_in, x_out, x_peer, carry_peer, slopes,
    feed, feed_rows, again, again_peer, hg, rg, hg_peer, rg_peer, late, r1, p2, ry, new,
    grads, grads_out, carry,
    load_sem, ss_send, ss_recv, first_send, first_recv, feed_send, feed_recv, again_send, again_recv,
    x_send, x_recv, peer_send, peer_recv, end_send, end_recv,
    rs_send, rs_recv, y_send, y_recv, ag_send, ag_recv, out_sem,
):
    inv_width = 1.0 / math.sqrt(D)
    inv_rank = BRANCH_SCALE / math.sqrt(RANK)
    s = lax.axis_index("pipe")
    dp = lax.axis_index("dp")
    c = lax.axis_index("mp")
    peer = 1 - c
    x = dp // 2
    yh = dp % 2
    y_other = x * 2 + 1 - yh
    is_first = s == 0
    is_last = s == sections - 1
    lag = 2 * sections - 1 - 2 * s
    late_section = lag < TICKS

    def remote(src, dst, send, recv, **where):
        return pltpu.make_async_remote_copy(
            src_ref=src, dst_ref=dst, send_sem=send, recv_sem=recv,
            device_id=where, device_id_type=MESH,
        )

    def landed(ref, sem):
        pltpu.make_async_copy(ref, ref, sem).wait()

    loads = [
        (fin, first.at[0, c]), (bin_, first.at[1, c]), (sq, w.at[0, c]), (ex, w.at[1, c]),
        (stash, st), (lsq, late.at[0]), (lex, late.at[1]),
    ]
    loads = [pltpu.make_async_copy(a, b, load_sem.at[i]) for i, (a, b) in enumerate(loads)]
    for load in loads:
        load.start()

    feed_tick = s // 4
    feed_group = (s % 4) // 2
    feed_core = s % 2
    own_feed = [is_first & (feed_core == c), is_last & (feed_core == c)]

    barrier = pltpu.get_barrier_semaphore()

    def hello(**where):
        pl.semaphore_signal(barrier, inc=1, device_id=where, device_id_type=MESH)

    hello(mp=peer)
    for d in range(1, 4):
        hello(dp=((x + d) % 4) * 2 + yh)
    hello(dp=y_other)

    @pl.when(s > 0)
    def _():
        hello(pipe=s - 1)

    @pl.when(s < sections - 1)
    def _():
        hello(pipe=s + 1)

    for at_end in (is_first, is_last):
        @pl.when(at_end)
        def _():
            def greet(i, _):
                who = (i // 2) * 2 + c
                core = i % 2

                @pl.when((who != s) | (core != c))
                def _():
                    hello(pipe=who, mp=core)

                return 0

            lax.fori_loop(0, sections, greet, 0)

    expected = (
        5 + (s > 0).astype(jnp.int32) + (s < sections - 1).astype(jnp.int32)
        + 1 - own_feed[0].astype(jnp.int32) + 1 - own_feed[1].astype(jnp.int32)
    )
    pl.semaphore_wait(barrier, expected)

    firsts = [
        remote(src, first.at[i, c], first_send.at[i], first_recv.at[i], mp=peer)
        for i, src in enumerate((fin, bin_))
    ]
    weights = [
        remote(src, w.at[i, c], ss_send.at[i], ss_recv.at[i], mp=peer)
        for i, src in enumerate((sq, ex))
    ]
    for copy in firsts + weights:
        copy.start()

    def send_feed():
        for k, (src, end) in enumerate(((act, 0), (cot, sections - 1))):
            slot = feed.at[feed_tick, feed_group, c]
            sem = feed_recv.at[feed_tick, feed_group, c]

            @pl.when(own_feed[k])
            def _():
                pltpu.make_async_copy(src, slot, sem).start()

            @pl.when(jnp.logical_not(own_feed[k]))
            def _():
                remote(src, slot, feed_send.at[k], sem, pipe=end, mp=feed_core).start()

    pl.when(feed_tick < 2)(send_feed)

    sources = (lsq, lex)
    owned = pl.ds(pl.multiple_of(16 * x, 16), 16)

    def x_at(d):
        return (x + d) % 4

    def sixteen(d):
        return pl.ds(pl.multiple_of(16 * x_at(d), 16), 16)

    def spread_late(h, d):
        return remote(
            sources[h].at[sixteen(d)], r1.at[h, d - 1], rs_send.at[h, d - 1], rs_recv.at[h, d - 1],
            dp=x_at(d) * 2 + yh)

    def exchange_late(h, part):
        cols = pl.ds(part * (half // 2), half // 2)
        return remote(
            p2.at[h, :, cols], ry.at[h, :, cols], y_send.at[h, part], y_recv.at[h, part], dp=y_other)

    def share_new(h, d):
        block = new.at[h, owned]
        return remote(
            block, block, ag_send.at[h, d - 1], ag_recv.at[h, d - 1], dp=x_at(d) * 2 + yh)

    def sum_late(h):
        total = late[h, owned, :].astype(F32)
        for d in range(1, 4):
            landed(r1.at[h, d - 1], rs_recv.at[h, d - 1])
        for d in range(1, 4):
            total = total + r1[h, d - 1].astype(F32)
        p2[h] = total.astype(BF16)

    def renew(h):
        for part in range(2):
            cols = pl.ds(part * (half // 2), half // 2)
            landed(ry.at[h, :, cols], y_recv.at[h, part])
        total = p2[h].astype(F32) + ry[h].astype(F32)
        old = w[h, c, owned, :].astype(F32)
        new[h, owned, :] = (old - STEP_RATE * total / replicas).astype(BF16)
        for d in range(1, 4):
            share_new(h, d).start()

    for h in range(2):
        for d in range(1, 4):
            spread_late(h, d).start()

    for i in (2, 4):
        loads[i].wait()
    own_squeeze = w[0, c]
    again[...] = rows_by_rows(st[...], jnp.concatenate([own_squeeze, own_squeeze], axis=0))
    again_copy = remote(again, again_peer, again_send, again_recv, mp=peer)
    again_copy.start()
    hg[...] = jnp.zeros_like(hg)
    rg[...] = jnp.zeros_like(rg)

    upper = lax.broadcasted_iota(jnp.int32, (GROUP, 2 * RANK), 0) < 4
    own_block = upper == (lax.broadcasted_iota(jnp.int32, (GROUP, 2 * RANK), 1) < RANK)
    own_rows = upper == (c == 0)
    upper_wide = lax.broadcasted_iota(jnp.int32, (GROUP, half), 0) < 4

    def crossed(w0, w1):
        w0 = w0.astype(F32)
        w1 = w1.astype(F32)
        low = jnp.where(upper_wide, w0, pltpu.roll(w1, 4, 0))
        high = jnp.where(upper_wide, pltpu.roll(w0, 4, 0), w1)
        return jnp.where(c == 0, low, high)

    loads[0].wait()
    loads[1].wait()
    for i in range(2):
        landed(first.at[i, peer], first_recv.at[i])
        w0 = first[i, 0].astype(F32)
        w1 = first[i, 1].astype(F32)
        for g in range(GROUPS):
            mine = slice(GROUP * g, GROUP * (g + 1))
            x_in[i, 0, g] = crossed(w0[mine], w1[mine]).astype(BF16)
    loads[3].wait()
    for i in range(2):
        landed(w.at[i, peer], ss_recv.at[i])

    def stacked(i):
        return w[i].reshape(2 * RANK, half)

    def both(v):
        return v + pltpu.roll(pltpu.roll(v, 4, 0), RANK, 1)

    def spread(v):
        return jnp.where(own_block, v, pltpu.roll(v, RANK, 1))

    def from_feed(tick, g, d):
        for h in range(2):
            landed(feed.at[tick, g, h], feed_recv.at[tick, g, h])
        for h in range(2):
            feed_rows[pl.ds(4 * h, 4), :] = feed[tick, g, h].astype(F32)
        x_in[d, tick, g] = feed_rows[pl.ds(0, GROUP), :].astype(BF16)

    def goes_on(d, tick):
        to = s + 1 - 2 * d
        return (tick < TICKS - 1) & (to >= 0) & (to < sections)

    def hop(d, tick, g):
        return remote(
            x_out.at[d, tick, g], x_in.at[d, tick + 1, g],
            x_send.at[d, tick, g], x_recv.at[d, tick + 1, g], pipe=s + 1 - 2 * d)

    def peer_copy(d, tick):
        return remote(
            x_in.at[d, tick], x_peer.at[d, tick], peer_send.at[d, tick], peer_recv.at[d, tick],
            mp=peer)

    def tile(tick, g):
        return pl.ds(pl.multiple_of(tick * ROWS + GROUP * g, GROUP), GROUP)

    def keep_hidden(tick, g, value):
        again[tile(tick + lag, g), :] = spread(value)

    def chain(d, tick, g, product, slope, keep=True):
        forward = d == 0
        value = both(product) * jnp.where(forward, inv_width, inv_rank)
        middle = jnp.where(forward, gelu(value), value * slope)
        middle = jnp.where(own_block, middle, 0.0).astype(BF16)
        branch = times(middle, stacked(1 - d)) * jnp.where(forward, inv_rank, inv_width)
        x_out[d, tick, g] = (x_in[d, tick, g].astype(F32) + branch).astype(BF16)

        @pl.when(goes_on(d, tick))
        def _():
            hop(d, tick, g).start()

        if keep:
            @pl.when(forward & (tick + lag < TICKS))
            def _():
                keep_hidden(tick, g, value)

        @pl.when(d == 1)
        def _():
            hg[tile(tick, g), :] = jnp.where(own_rows, spread(middle.astype(F32)), 0.0)

        return value

    def recomputed(tick, g):
        seen = again[tile(tick, g), :]
        seen = jnp.where(own_rows, seen, pltpu.roll(seen, 4, 0))
        rg[tile(tick, g), :] = jnp.where(own_rows, gelu(seen).astype(BF16).astype(F32), 0.0)
        return gelu_slope(seen)

    def after(tick):
        peer_copy(1, tick).start()

        @pl.when(late_section)
        def _():
            peer_copy(0, tick).start()

        @pl.when(feed_tick == tick + 2)
        def _():
            send_feed()

    for g in range(GROUPS):
        @pl.when(is_first)
        def _():
            from_feed(0, g, 0)

        hidden = chain(0, 0, g, rows_by_rows(x_in[0, 0, g], stacked(0)), 0.0, keep=False)
        if g == 0:
            again_copy.wait()
            again[...] = (again[...] + again_peer[...]) * inv_width

        @pl.when(lag < TICKS)
        def _():
            keep_hidden(0, g, hidden)

        @pl.when(is_last)
        def _():
            from_feed(0, g, 1)

        chain(1, 0, g, rows_by_rows(x_in[1, 0, g], stacked(1)), recomputed(0, g))
    after(0)
    for k in range(7):
        some = pl.ds(k * (half // 7), half // 7)
        for i in range(2):
            cols[i, some, :] = jnp.transpose(w[i, :, :, some].reshape(2 * RANK, half // 7))
    loads[5].wait()
    loads[6].wait()

    rg_copy = remote(rg, rg_peer, end_send.at[1], end_recv.at[1], mp=peer)

    def tick_body(tick, _):
        for g in range(GROUPS):
            slopes[g] = recomputed(tick, g)
        @pl.when(tick == TICKS - 1)
        def _():
            rg_copy.start()

        for h in range(2):
            for part in range(2):
                @pl.when(tick == EXCHANGE_TICKS[h][part] + 1)
                def _():
                    exchange_late(h, part).start()

        turned = (s % 8 < tick).astype(jnp.int32)

        def slot(n, _):
            g = n // 2
            d = turned + (n % 2) * (1 - 2 * turned)
            fed = (is_first & (d == 0)) | (is_last & (d == 1))

            @pl.when(fed)
            def _():
                from_feed(tick, g, d)

            @pl.when(jnp.logical_not(fed))
            def _():
                landed(x_in.at[d, tick, g], x_recv.at[d, tick, g])

            chain(d, tick, g, times(x_in[d, tick, g], cols[d]), slopes[g])
            return 0

        lax.fori_loop(0, 2 * GROUPS, slot, 0)
        after(tick)
        @pl.when(tick == SUM_TICK)
        def _():
            for h in range(2):
                sum_late(h)

        for h in range(2):
            @pl.when(tick == RENEW_TICKS[h])
            def _():
                renew(h)

        return 0

    lax.fori_loop(1, TICKS, tick_body, 0)

    hg_copy = remote(hg, hg_peer, end_send.at[0], end_recv.at[0], mp=peer)
    carries = [
        remote(
            x_out.at[i, TICKS - 1], carry_peer.at[i], end_send.at[2 + i], end_recv.at[2 + i], mp=peer)
        for i in range(2)
    ]
    hg_copy.start()
    for copy in carries:
        copy.start()
    outs = []

    def put(src, dst):
        copy = pltpu.make_async_copy(src, dst, out_sem.at[len(outs)])
        copy.start()
        outs.append(copy)


    def swapped_rows(v):
        v = v.reshape(-1, 2, 4, 2 * RANK)
        return jnp.concatenate([v[:, 1:], v[:, :1]], axis=1).reshape(-1, 2 * RANK)

    def as_left(v):
        return jnp.transpose(v)[:RANK].astype(BF16)

    def all_ticks(ref):
        return ref.reshape(TICKS * ROWS, half)

    grads[...] = times(as_left(rg[...]), all_ticks(x_in[1]))
    rg_copy.wait()
    peer_left = as_left(swapped_rows(rg_peer[...]))
    for tick in range(TICKS):
        peer_copy(1, tick).wait()
    grads_out[1] = (inv_rank * (grads[...] + times(peer_left, all_ticks(x_peer[1])))).astype(BF16)
    put(grads_out.at[1], gex)

    hg_copy.wait()
    total_hg = hg[...] + hg_peer[...]
    row = lax.broadcasted_iota(jnp.int32, (TICKS * ROWS, 2 * RANK), 0)
    left = as_left(jnp.where(row < lag * ROWS, total_hg, 0.0))
    grads[...] = times(left, st[...])

    @pl.when(late_section)
    def _():
        for tick in range(TICKS):
            peer_copy(0, tick).wait()
        moved = []
        for ref, swap in ((hg, False), (hg_peer, True)):
            pieces = []
            for tick in range(TICKS):
                source = jnp.minimum(tick + lag, TICKS - 1)
                piece = ref[pl.ds(pl.multiple_of(source * ROWS, ROWS), ROWS), :]
                if swap:
                    piece = swapped_rows(piece)
                pieces.append(jnp.where(tick + lag < TICKS, piece, 0.0))
            moved.append(as_left(jnp.concatenate(pieces, axis=0)))
        grads[...] = (
            grads[...] + times(moved[0], all_ticks(x_in[0])) + times(moved[1], all_ticks(x_peer[0]))
        )

    grads_out[0] = (inv_width * grads[...]).astype(BF16)
    put(grads_out.at[0], gsq)

    for copy in carries:
        copy.wait()
    for i, out in enumerate((fco, bco)):
        for g in range(GROUPS):
            mine = x_out[i, TICKS - 1, g].astype(F32)
            other = carry_peer[i, g].astype(F32)
            feed_rows[pl.ds(GROUP * g, GROUP), :] = crossed(
                jnp.where(c == 0, mine, other), jnp.where(c == 0, other, mine))
        carry[i] = feed_rows[...].astype(BF16)
        put(carry.at[i], out)

    for h, out in enumerate((nsq, nex)):
        for d in range(1, 4):
            landed(new.at[h, sixteen(4 - d)], ag_recv.at[h, d - 1])
        put(new.at[h], out)

    for copy in firsts + weights:
        copy.wait_send()
    for k, (src, end) in enumerate(((act, 0), (cot, sections - 1))):
        @pl.when(jnp.logical_not(own_feed[k]))
        def _():
            remote(
                src, feed.at[feed_tick, feed_group, c], feed_send.at[k],
                feed_recv.at[feed_tick, feed_group, c], pipe=end, mp=feed_core,
            ).wait_send()
    for h in range(2):
        for d in range(1, 4):
            spread_late(h, d).wait_send()
            share_new(h, d).wait_send()
        for part in range(2):
            exchange_late(h, part).wait_send()

    def sent(tick, _):
        for g in range(GROUPS):
            for d in range(2):
                @pl.when(goes_on(d, tick))
                def _():
                    hop(d, tick, g).wait_send()

        return 0

    lax.fori_loop(0, TICKS - 1, sent, 0)
    for copy in outs:
        copy.wait()


def put_out(*refs):
    sources, outs, held, sems = refs[:6], refs[6:12], refs[12:18], refs[18]
    steps = []
    for i in range(6):
        size = 32 if i < 4 else 16
        for start in range(0, outs[i].shape[0], size):
            rows = pl.ds(start, size)
            n = len(steps)
            steps.append((
                pltpu.make_async_copy(sources[i].at[rows], held[i].at[rows], sems.at[0, n]),
                pltpu.make_async_copy(held[i].at[rows], outs[i].at[rows], sems.at[1, n]),
            ))
    for load, _ in steps:
        load.start()
    for load, store in steps:
        load.wait()
        store.start()
    for _, store in steps:
        store.wait()


def shards(
    activations, cotangent, squeeze_old, expand_old, squeeze_late, expand_late,
    stash_inputs, forward_in, backward_in,
):
    sections = lax.axis_size("pipe")
    replicas = lax.axis_size("dp")
    half = squeeze_old.shape[1]
    vmem = pltpu.VMEM
    dma = pltpu.SemaphoreType.DMA
    ticked = vmem((2, TICKS, GROUPS, GROUP, half), BF16)
    small = vmem((TICKS * ROWS, 2 * RANK), F32)
    hbm_spec = pl.BlockSpec(memory_space=pltpu.HBM)
    outs = pl.pallas_call(
        functools.partial(window, sections, replicas, half),
        out_shape=[jax.ShapeDtypeStruct((RANK, half), BF16)] * 4
        + [jax.ShapeDtypeStruct((ROWS, half), BF16)] * 2,
        in_specs=[hbm_spec] * 9,
        out_specs=[hbm_spec] * 6,
        scratch_shapes=[
            vmem((2, 2, RANK, half), BF16),
            vmem((TICKS * ROWS, half), BF16),
            vmem((2, 2, ROWS, half), BF16),
            vmem((2, half, 2 * RANK), BF16),
            ticked, ticked, ticked,
            vmem((2, GROUPS, GROUP, half), BF16),
            vmem((GROUPS, GROUP, 2 * RANK), F32),
            vmem((TICKS, GROUPS, 2, 4, half), BF16),
            vmem((ROWS, half), F32),
            small, small, small, small, small, small,
            vmem((2, RANK, half), BF16),
            vmem((2, 3, 16, half), BF16),
            vmem((2, 16, half), BF16),
            vmem((2, 16, half), BF16),
            vmem((2, RANK, half), BF16),
            vmem((RANK, half), F32),
            vmem((2, RANK, half), BF16),
            vmem((2, ROWS, half), BF16),
            dma((7,)),
            dma((2,)), dma((2,)),
            dma((2,)), dma((2,)),
            dma((2,)), dma((TICKS, GROUPS, 2)),
            dma, dma,
            dma((2, TICKS, GROUPS)), dma((2, TICKS, GROUPS)),
            dma((2, TICKS)), dma((2, TICKS)),
            dma((4,)), dma((4,)),
            dma((2, 3)), dma((2, 3)), dma((2, 2)), dma((2, 2)), dma((2, 3)), dma((2, 3)),
            dma((6,)),
        ],
        compiler_params=pltpu.CompilerParams(
            collective_id=0, has_side_effects=True, vmem_limit_bytes=62 * 1024 * 1024
        ),
        name="window",
    )(
        activations[0], cotangent[0], squeeze_old[0].T, expand_old[0],
        squeeze_late[0, 0].T, expand_late[0, 0], stash_inputs[0, 0].reshape(TICKS * ROWS, half),
        forward_in[0, 0], backward_in[0, 0],
    )
    nsq, nex, gsq, gex, fco, bco = pl.pallas_call(
        put_out,
        out_shape=[jax.ShapeDtypeStruct(out.shape, out.dtype) for out in outs],
        in_specs=[hbm_spec] * 6,
        out_specs=[hbm_spec] * 6,
        scratch_shapes=[vmem(out.shape, out.dtype) for out in outs] + [dma((2, 10))],
        compiler_params=pltpu.CompilerParams(vmem_limit_bytes=62 * 1024 * 1024),
        name="put_out",
    )(*outs)
    return (
        nsq.T[None], nex[None], gsq.T[None, None], gex[None, None],
        fco[None, None], bco[None, None],
    )


def solution(mesh):
    placed = (
        P("dp", "pipe", "mp"),
        P("dp", "pipe", "mp"),
        P("pipe", "mp", None),
        P("pipe", None, "mp"),
        P("dp", "pipe", "mp", None),
        P("dp", "pipe", None, "mp"),
        P("dp", "pipe", None, None, "mp"),
        P("dp", "pipe", None, "mp"),
        P("dp", "pipe", None, "mp"),
    )
    return jax.shard_map(
        shards,
        mesh=mesh,
        in_specs=placed,
        out_specs=(
            P("pipe", "mp", None),
            P("pipe", None, "mp"),
            P("dp", "pipe", "mp", None),
            P("dp", "pipe", None, "mp"),
            P("dp", "pipe", None, "mp"),
            P("dp", "pipe", None, "mp"),
        ),
        check_vma=False,
    )
```

```python
import functools
import math

import jax
import jax.numpy as jnp
from jax import lax
from jax.experimental import pallas as pl
from jax.experimental.pallas import tpu as pltpu
from jax.sharding import PartitionSpec as P

D = 7168
RANK = 64
TICKS = 8
ROWS = 16
BRANCH_SCALE = 0.25
STEP_RATE = 0.5
GROUPS = 2
GROUP = 8
SUM_TICK = 1
EXCHANGE_TICKS = ((1, 2), (3, 4))
RENEW_TICKS = (4, 6)

F32 = jnp.float32
BF16 = jnp.bfloat16
MESH = pl.DeviceIdType.MESH
GELU_A = math.sqrt(2.0 / math.pi)
GELU_B = 0.044715


def gelu(v):
    return 0.5 * v * (1.0 + jnp.tanh(GELU_A * (v + GELU_B * (v * v * v))))


def gelu_slope(v):
    t = jnp.tanh(GELU_A * (v + GELU_B * (v * v * v)))
    inner = GELU_A * (1.0 + 3.0 * GELU_B * (v * v))
    return 0.5 * (1.0 + t) + 0.5 * v * ((1.0 - t * t) * inner)


def rows_by_rows(left, right):
    return lax.dot_general(left, right, (((1,), (1,)), ((), ())), preferred_element_type=F32)


def times(left, right):
    return jnp.dot(left, right, preferred_element_type=F32)


def window(
    sections, replicas, half,
    act, cot, sq, ex, lsq, lex, stash, fin, bin_,
    nsq, nex, gsq, gex, fco, bco,
    w, st, first, cols, x_in, x_out, x_peer, carry_peer, slopes,
    feed, feed_rows, again, again_peer, hg, rg, hg_peer, rg_peer, late, r1, p2, ry, new,
    grads, grads_out, carry,
    load_sem, ss_send, ss_recv, first_send, first_recv, feed_send, feed_recv, again_send, again_recv,
    x_send, x_recv, peer_send, peer_recv, end_send, end_recv,
    rs_send, rs_recv, y_send, y_recv, ag_send, ag_recv, out_sem,
):
    inv_width = 1.0 / math.sqrt(D)
    inv_rank = BRANCH_SCALE / math.sqrt(RANK)
    s = lax.axis_index("pipe")
    dp = lax.axis_index("dp")
    c = lax.axis_index("mp")
    peer = 1 - c
    x = dp // 2
    yh = dp % 2
    y_other = x * 2 + 1 - yh
    is_first = s == 0
    is_last = s == sections - 1
    lag = 2 * sections - 1 - 2 * s
    late_section = lag < TICKS

    def remote(src, dst, send, recv, **where):
        return pltpu.make_async_remote_copy(
            src_ref=src, dst_ref=dst, send_sem=send, recv_sem=recv,
            device_id=where, device_id_type=MESH,
        )

    def landed(ref, sem):
        pltpu.make_async_copy(ref, ref, sem).wait()

    feed_tick = s // 4
    feed_group = (s % 4) // 2
    feed_core = s % 2
    own_feed = [is_first & (feed_core == c), is_last & (feed_core == c)]

    barrier = pltpu.get_barrier_semaphore()

    def hello(**where):
        pl.semaphore_signal(barrier, inc=1, device_id=where, device_id_type=MESH)

    for end, at_end in enumerate((is_first, is_last)):
        @pl.when(at_end)
        def _():
            for i in range(sections):
                who = (i // 2) * 2 + c
                core = i % 2
                if i == end * (sections - 1):
                    @pl.when((who != s) | (core != c))
                    def _():
                        hello(pipe=who, mp=core)
                else:
                    hello(pipe=who, mp=core)

    hello(mp=peer)
    for d in range(1, 4):
        hello(dp=((x + d) % 4) * 2 + yh)
    hello(dp=y_other)

    @pl.when(s > 0)
    def _():
        hello(pipe=s - 1)

    @pl.when(s < sections - 1)
    def _():
        hello(pipe=s + 1)

    loads = [
        (fin, first.at[0, c]), (bin_, first.at[1, c]), (sq, w.at[0, c]), (ex, w.at[1, c]),
        (stash, st), (lsq, late.at[0]), (lex, late.at[1]),
    ]
    loads = [pltpu.make_async_copy(a, b, load_sem.at[i]) for i, (a, b) in enumerate(loads)]
    for load in loads[:5]:
        load.start()

    expected = (
        5 + (s > 0).astype(jnp.int32) + (s < sections - 1).astype(jnp.int32)
        + 1 - own_feed[0].astype(jnp.int32) + 1 - own_feed[1].astype(jnp.int32)
    )
    pl.semaphore_wait(barrier, expected)

    firsts = [
        remote(src, first.at[i, c], first_send.at[i], first_recv.at[i], mp=peer)
        for i, src in enumerate((fin, bin_))
    ]
    weights = [
        remote(src, w.at[i, c], ss_send.at[i], ss_recv.at[i], mp=peer)
        for i, src in enumerate((sq, ex))
    ]
    for copy in firsts + weights:
        copy.start()

    def send_feed():
        for k, (src, end) in enumerate(((act, 0), (cot, sections - 1))):
            slot = feed.at[feed_tick, feed_group, c]
            sem = feed_recv.at[feed_tick, feed_group, c]

            @pl.when(own_feed[k])
            def _():
                pltpu.make_async_copy(src, slot, sem).start()

            @pl.when(jnp.logical_not(own_feed[k]))
            def _():
                remote(src, slot, feed_send.at[k], sem, pipe=end, mp=feed_core).start()

    pl.when(feed_tick < 2)(send_feed)

    sources = (lsq, lex)
    owned = pl.ds(pl.multiple_of(16 * x, 16), 16)

    def x_at(d):
        return (x + d) % 4

    def sixteen(d):
        return pl.ds(pl.multiple_of(16 * x_at(d), 16), 16)

    def spread_late(h, d):
        return remote(
            sources[h].at[sixteen(d)], r1.at[h, d - 1], rs_send.at[h, d - 1], rs_recv.at[h, d - 1],
            dp=x_at(d) * 2 + yh)

    def exchange_late(h, part):
        cols = pl.ds(part * (half // 2), half // 2)
        return remote(
            p2.at[h, :, cols], ry.at[h, :, cols], y_send.at[h, part], y_recv.at[h, part], dp=y_other)

    def share_new(h, d):
        block = new.at[h, owned]
        return remote(
            block, block, ag_send.at[h, d - 1], ag_recv.at[h, d - 1], dp=x_at(d) * 2 + yh)

    def sum_late(h):
        total = late[h, owned, :].astype(F32)
        for d in range(1, 4):
            landed(r1.at[h, d - 1], rs_recv.at[h, d - 1])
        for d in range(1, 4):
            total = total + r1[h, d - 1].astype(F32)
        p2[h] = total.astype(BF16)

    def renew(h):
        for part in range(2):
            cols = pl.ds(part * (half // 2), half // 2)
            landed(ry.at[h, :, cols], y_recv.at[h, part])
        total = p2[h].astype(F32) + ry[h].astype(F32)
        old = w[h, c, owned, :].astype(F32)
        new[h, owned, :] = (old - STEP_RATE * total / replicas).astype(BF16)
        for d in range(1, 4):
            share_new(h, d).start()

    for h in range(2):
        for d in range(1, 4):
            spread_late(h, d).start()

    for i in (2, 4):
        loads[i].wait()
    own_squeeze = w[0, c]
    again[...] = rows_by_rows(st[...], jnp.concatenate([own_squeeze, own_squeeze], axis=0))
    again_copy = remote(again, again_peer, again_send, again_recv, mp=peer)
    again_copy.start()
    hg[...] = jnp.zeros_like(hg)
    rg[...] = jnp.zeros_like(rg)

    upper = lax.broadcasted_iota(jnp.int32, (GROUP, 2 * RANK), 0) < 4
    own_block = upper == (lax.broadcasted_iota(jnp.int32, (GROUP, 2 * RANK), 1) < RANK)
    own_rows = upper == (c == 0)
    upper_wide = lax.broadcasted_iota(jnp.int32, (GROUP, half), 0) < 4

    def crossed(w0, w1):
        w0 = w0.astype(F32)
        w1 = w1.astype(F32)
        low = jnp.where(upper_wide, w0, pltpu.roll(w1, 4, 0))
        high = jnp.where(upper_wide, pltpu.roll(w0, 4, 0), w1)
        return jnp.where(c == 0, low, high)

    loads[0].wait()
    loads[1].wait()
    for i in range(2):
        landed(first.at[i, peer], first_recv.at[i])
        w0 = first[i, 0].astype(F32)
        w1 = first[i, 1].astype(F32)
        for g in range(GROUPS):
            mine = slice(GROUP * g, GROUP * (g + 1))
            x_in[i, 0, g] = crossed(w0[mine], w1[mine]).astype(BF16)
    loads[3].wait()
    for i in range(2):
        landed(w.at[i, peer], ss_recv.at[i])

    def stacked(i):
        return w[i].reshape(2 * RANK, half)

    def both(v):
        return v + pltpu.roll(pltpu.roll(v, 4, 0), RANK, 1)

    def spread(v):
        return jnp.where(own_block, v, pltpu.roll(v, RANK, 1))

    def from_feed(tick, g, d):
        for h in range(2):
            landed(feed.at[tick, g, h], feed_recv.at[tick, g, h])
        for h in range(2):
            feed_rows[pl.ds(4 * h, 4), :] = feed[tick, g, h].astype(F32)
        x_in[d, tick, g] = feed_rows[pl.ds(0, GROUP), :].astype(BF16)

    def goes_on(d, tick):
        to = s + 1 - 2 * d
        return (tick < TICKS - 1) & (to >= 0) & (to < sections)

    def hop(d, tick, g):
        return remote(
            x_out.at[d, tick, g], x_in.at[d, tick + 1, g],
            x_send.at[d, tick, g], x_recv.at[d, tick + 1, g], pipe=s + 1 - 2 * d)

    def peer_copy(d, tick):
        return remote(
            x_in.at[d, tick], x_peer.at[d, tick], peer_send.at[d, tick], peer_recv.at[d, tick],
            mp=peer)

    def tile(tick, g):
        return pl.ds(pl.multiple_of(tick * ROWS + GROUP * g, GROUP), GROUP)

    def keep_hidden(tick, g, value):
        again[tile(tick + lag, g), :] = spread(value)

    def chain(d, tick, g, product, slope, keep=True):
        forward = d == 0
        value = both(product) * jnp.where(forward, inv_width, inv_rank)
        middle = jnp.where(forward, gelu(value), value * slope)
        middle = jnp.where(own_block, middle, 0.0).astype(BF16)
        branch = times(middle, stacked(1 - d)) * jnp.where(forward, inv_rank, inv_width)
        x_out[d, tick, g] = (x_in[d, tick, g].astype(F32) + branch).astype(BF16)

        @pl.when(goes_on(d, tick))
        def _():
            hop(d, tick, g).start()

        if keep:
            @pl.when(forward & (tick + lag < TICKS))
            def _():
                keep_hidden(tick, g, value)

        @pl.when(d == 1)
        def _():
            hg[tile(tick, g), :] = jnp.where(own_rows, spread(middle.astype(F32)), 0.0)

        return value

    def recomputed(tick, g):
        seen = again[tile(tick, g), :]
        seen = jnp.where(own_rows, seen, pltpu.roll(seen, 4, 0))
        rg[tile(tick, g), :] = jnp.where(own_rows, gelu(seen).astype(BF16).astype(F32), 0.0)
        return gelu_slope(seen)

    def after(tick):
        peer_copy(1, tick).start()

        @pl.when(late_section)
        def _():
            peer_copy(0, tick).start()

        @pl.when(feed_tick == tick + 2)
        def _():
            send_feed()

    for load in loads[5:]:
        load.start()

    def first_product(d):
        both_groups = [x_in[d, 0, g].astype(F32) for g in range(GROUPS)]
        product = rows_by_rows(jnp.concatenate(both_groups, axis=0).astype(BF16), stacked(d))
        return [product[GROUP * g:GROUP * (g + 1)] for g in range(GROUPS)]

    for g in range(GROUPS):
        @pl.when(is_first)
        def _():
            from_feed(0, g, 0)

        @pl.when(is_last)
        def _():
            from_feed(0, g, 1)

    product = first_product(0)
    hidden = [chain(0, 0, g, product[g], 0.0, keep=False) for g in range(GROUPS)]
    product = first_product(1)
    again_copy.wait()
    again[...] = (again[...] + again_peer[...]) * inv_width

    @pl.when(lag < TICKS)
    def _():
        for g in range(GROUPS):
            keep_hidden(0, g, hidden[g])

    for g in range(GROUPS):
        chain(1, 0, g, product[g], recomputed(0, g))
    after(0)
    for k in range(7):
        some = pl.ds(k * (half // 7), half // 7)
        for i in range(2):
            cols[i, some, :] = jnp.transpose(w[i, :, :, some].reshape(2 * RANK, half // 7))
    loads[5].wait()
    loads[6].wait()

    rg_copy = remote(rg, rg_peer, end_send.at[1], end_recv.at[1], mp=peer)

    def tick_body(tick, _):
        for g in range(GROUPS):
            slopes[g] = recomputed(tick, g)
        @pl.when(tick == TICKS - 1)
        def _():
            rg_copy.start()

        for h in range(2):
            for part in range(2):
                @pl.when(tick == EXCHANGE_TICKS[h][part] + 1)
                def _():
                    exchange_late(h, part).start()

        turned = (s % 8 < tick).astype(jnp.int32)

        def slot(n, _):
            g = n // 2
            d = turned + (n % 2) * (1 - 2 * turned)
            fed = (is_first & (d == 0)) | (is_last & (d == 1))

            @pl.when(fed)
            def _():
                from_feed(tick, g, d)

            @pl.when(jnp.logical_not(fed))
            def _():
                landed(x_in.at[d, tick, g], x_recv.at[d, tick, g])

            chain(d, tick, g, times(x_in[d, tick, g], cols[d]), slopes[g])
            return 0

        lax.fori_loop(0, 2 * GROUPS, slot, 0)
        after(tick)
        @pl.when(tick == SUM_TICK)
        def _():
            for h in range(2):
                sum_late(h)

        for h in range(2):
            @pl.when(tick == RENEW_TICKS[h])
            def _():
                renew(h)

        return 0

    lax.fori_loop(1, TICKS, tick_body, 0)

    hg_copy = remote(hg, hg_peer, end_send.at[0], end_recv.at[0], mp=peer)
    carries = [
        remote(
            x_out.at[i, TICKS - 1], carry_peer.at[i], end_send.at[2 + i], end_recv.at[2 + i], mp=peer)
        for i in range(2)
    ]
    hg_copy.start()
    for copy in carries:
        copy.start()
    outs = []

    def put(src, dst):
        copy = pltpu.make_async_copy(src, dst, out_sem.at[len(outs)])
        copy.start()
        outs.append(copy)


    def swapped_rows(v):
        v = v.reshape(-1, 2, 4, 2 * RANK)
        return jnp.concatenate([v[:, 1:], v[:, :1]], axis=1).reshape(-1, 2 * RANK)

    def as_left(v):
        return jnp.transpose(v)[:RANK].astype(BF16)

    def all_ticks(ref):
        return ref.reshape(TICKS * ROWS, half)

    def put_new(h, out):
        for d in range(1, 4):
            landed(new.at[h, sixteen(4 - d)], ag_recv.at[h, d - 1])
        put(new.at[h], out)

    put_new(0, nsq)
    grads[...] = times(as_left(rg[...]), all_ticks(x_in[1]))
    rg_copy.wait()
    peer_left = as_left(swapped_rows(rg_peer[...]))
    for tick in range(TICKS):
        peer_copy(1, tick).wait()
    grads_out[1] = (inv_rank * (grads[...] + times(peer_left, all_ticks(x_peer[1])))).astype(BF16)
    put(grads_out.at[1], gex)

    hg_copy.wait()
    total_hg = hg[...] + hg_peer[...]
    row = lax.broadcasted_iota(jnp.int32, (TICKS * ROWS, 2 * RANK), 0)
    left = as_left(jnp.where(row < lag * ROWS, total_hg, 0.0))
    grads[...] = times(left, st[...])

    @pl.when(late_section)
    def _():
        for tick in range(TICKS):
            peer_copy(0, tick).wait()
        moved = []
        for ref, swap in ((hg, False), (hg_peer, True)):
            pieces = []
            for tick in range(TICKS):
                source = jnp.minimum(tick + lag, TICKS - 1)
                piece = ref[pl.ds(pl.multiple_of(source * ROWS, ROWS), ROWS), :]
                if swap:
                    piece = swapped_rows(piece)
                pieces.append(jnp.where(tick + lag < TICKS, piece, 0.0))
            moved.append(as_left(jnp.concatenate(pieces, axis=0)))
        grads[...] = (
            grads[...] + times(moved[0], all_ticks(x_in[0])) + times(moved[1], all_ticks(x_peer[0]))
        )

    grads_out[0] = (inv_width * grads[...]).astype(BF16)
    put(grads_out.at[0], gsq)

    for copy in carries:
        copy.wait()
    for i, out in enumerate((fco, bco)):
        for g in range(GROUPS):
            mine = x_out[i, TICKS - 1, g].astype(F32)
            other = carry_peer[i, g].astype(F32)
            feed_rows[pl.ds(GROUP * g, GROUP), :] = crossed(
                jnp.where(c == 0, mine, other), jnp.where(c == 0, other, mine))
        carry[i] = feed_rows[...].astype(BF16)
        put(carry.at[i], out)

    put_new(1, nex)

    for copy in firsts + weights:
        copy.wait_send()
    for k, (src, end) in enumerate(((act, 0), (cot, sections - 1))):
        @pl.when(jnp.logical_not(own_feed[k]))
        def _():
            remote(
                src, feed.at[feed_tick, feed_group, c], feed_send.at[k],
                feed_recv.at[feed_tick, feed_group, c], pipe=end, mp=feed_core,
            ).wait_send()
    for h in range(2):
        for d in range(1, 4):
            spread_late(h, d).wait_send()
            share_new(h, d).wait_send()
        for part in range(2):
            exchange_late(h, part).wait_send()

    def sent(tick, _):
        for g in range(GROUPS):
            for d in range(2):
                @pl.when(goes_on(d, tick))
                def _():
                    hop(d, tick, g).wait_send()

        return 0

    lax.fori_loop(0, TICKS - 1, sent, 0)
    for copy in outs:
        copy.wait()


def put_out(*refs):
    sources, outs, held, sems = refs[:6], refs[6:12], refs[12:18], refs[18]
    steps = []
    for i in range(6):
        size = 32 if i < 4 else 16
        for start in range(0, outs[i].shape[0], size):
            rows = pl.ds(start, size)
            n = len(steps)
            steps.append((
                pltpu.make_async_copy(sources[i].at[rows], held[i].at[rows], sems.at[0, n]),
                pltpu.make_async_copy(held[i].at[rows], outs[i].at[rows], sems.at[1, n]),
            ))
    for load, _ in steps:
        load.start()
    for load, store in steps:
        load.wait()
        store.start()
    for _, store in steps:
        store.wait()


def shards(
    activations, cotangent, squeeze_old, expand_old, squeeze_late, expand_late,
    stash_inputs, forward_in, backward_in,
):
    sections = lax.axis_size("pipe")
    replicas = lax.axis_size("dp")
    half = squeeze_old.shape[1]
    vmem = pltpu.VMEM
    dma = pltpu.SemaphoreType.DMA
    ticked = vmem((2, TICKS, GROUPS, GROUP, half), BF16)
    small = vmem((TICKS * ROWS, 2 * RANK), F32)
    hbm_spec = pl.BlockSpec(memory_space=pltpu.HBM)
    outs = pl.pallas_call(
        functools.partial(window, sections, replicas, half),
        out_shape=[jax.ShapeDtypeStruct((RANK, half), BF16)] * 4
        + [jax.ShapeDtypeStruct((ROWS, half), BF16)] * 2,
        in_specs=[hbm_spec] * 9,
        out_specs=[hbm_spec] * 6,
        scratch_shapes=[
            vmem((2, 2, RANK, half), BF16),
            vmem((TICKS * ROWS, half), BF16),
            vmem((2, 2, ROWS, half), BF16),
            vmem((2, half, 2 * RANK), BF16),
            ticked, ticked, ticked,
            vmem((2, GROUPS, GROUP, half), BF16),
            vmem((GROUPS, GROUP, 2 * RANK), F32),
            vmem((TICKS, GROUPS, 2, 4, half), BF16),
            vmem((ROWS, half), F32),
            small, small, small, small, small, small,
            vmem((2, RANK, half), BF16),
            vmem((2, 3, 16, half), BF16),
            vmem((2, 16, half), BF16),
            vmem((2, 16, half), BF16),
            vmem((2, RANK, half), BF16),
            vmem((RANK, half), F32),
            vmem((2, RANK, half), BF16),
            vmem((2, ROWS, half), BF16),
            dma((7,)),
            dma((2,)), dma((2,)),
            dma((2,)), dma((2,)),
            dma((2,)), dma((TICKS, GROUPS, 2)),
            dma, dma,
            dma((2, TICKS, GROUPS)), dma((2, TICKS, GROUPS)),
            dma((2, TICKS)), dma((2, TICKS)),
            dma((4,)), dma((4,)),
            dma((2, 3)), dma((2, 3)), dma((2, 2)), dma((2, 2)), dma((2, 3)), dma((2, 3)),
            dma((6,)),
        ],
        compiler_params=pltpu.CompilerParams(
            collective_id=0, has_side_effects=True, vmem_limit_bytes=62 * 1024 * 1024
        ),
        name="window",
    )(
        activations[0], cotangent[0], squeeze_old[0].T, expand_old[0],
        squeeze_late[0, 0].T, expand_late[0, 0], stash_inputs[0, 0].reshape(TICKS * ROWS, half),
        forward_in[0, 0], backward_in[0, 0],
    )
    nsq, nex, gsq, gex, fco, bco = pl.pallas_call(
        put_out,
        out_shape=[jax.ShapeDtypeStruct(out.shape, out.dtype) for out in outs],
        in_specs=[hbm_spec] * 6,
        out_specs=[hbm_spec] * 6,
        scratch_shapes=[vmem(out.shape, out.dtype) for out in outs] + [dma((2, 10))],
        compiler_params=pltpu.CompilerParams(vmem_limit_bytes=62 * 1024 * 1024),
        name="put_out",
    )(*outs)
    return (
        nsq.T[None], nex[None], gsq.T[None, None], gex[None, None],
        fco[None, None], bco[None, None],
    )


def solution(mesh):
    placed = (
        P("dp", "pipe", "mp"),
        P("dp", "pipe", "mp"),
        P("pipe", "mp", None),
        P("pipe", None, "mp"),
        P("dp", "pipe", "mp", None),
        P("dp", "pipe", None, "mp"),
        P("dp", "pipe", None, None, "mp"),
        P("dp", "pipe", None, "mp"),
        P("dp", "pipe", None, "mp"),
    )
    return jax.shard_map(
        shards,
        mesh=mesh,
        in_specs=placed,
        out_specs=(
            P("pipe", "mp", None),
            P("pipe", None, "mp"),
            P("dp", "pipe", "mp", None),
            P("dp", "pipe", None, "mp"),
            P("dp", "pipe", None, "mp"),
            P("dp", "pipe", None, "mp"),
        ),
        check_vma=False,
    )
```
